256 devices in a mesh: chan: 4 (over x_lo, core), pair: 16 (over z, x_hi), tm: 4 (over y).
Axes of the slice: x: 4 (x_hi: 2, x_lo: 2; x = x_hi * 2 + x_lo), y: 4, z: 8, core: 2. Of those that a mesh axis runs over, the one named last changes fastest.
Arguments:
- voltages: bfloat16 [16, 128, 524288], P('pair', 'chan', 'tm'), may hold values from -127 to 127, as said below
- selected: int32 [32], replicated, may hold values from 0 to 1023, as said below
Outputs:
- visibility: float32 [2, 32, 2048, 2048], P(None, 'chan', 'pair', 'tm')
The draws below stay inside these ranges and needn't reach their ends.
Inputs may be any that keep to these rules, and one draw needn't show every extreme that they name: `voltages`: whole numbers. `selected`: 32 different channel numbers; channels 0 and 1023 are always among them.
All inputs are finite; a program needn't handle non-finite values.
Results may differ from the reference program's by a relative error of at most 0.013.
Values may be sent and summed in bfloat16 or wider, within the bound.
No kernel may reach another device: no remote copies, remote signals or barrier semaphores. Data moves between devices by JAX's collectives and lax.ppermute only.
A program may use at most 128 MiB of HBM per device.

```python
import math
import jax
import jax.numpy as jnp
from jax import lax

INPUTS = 2048
NFFT = 2048
TAPS = 4
NSEL = 32
NCHAN = 1024
BLOCKS = 16
BLOCK = 128
SPECTRA = 256
SAMPLES = 524288


def draw_voltages(key, part):
    key = jax.random.fold_in(key, 11)
    noise_key = jax.random.fold_in(key, 0)
    dims = (BLOCKS, BLOCK, SAMPLES)
    values = 24.0 * jax.random.normal(noise_key, dims)
    return jnp.clip(jnp.floor(values + 0.5), -127.0, 127.0).astype(jnp.bfloat16)


def draw_selected(key, part):
    key = jax.random.fold_in(key, 23)
    first_key, second_key = jax.random.split(key, 2)
    middle = jax.random.permutation(first_key, NCHAN - 2)[:NSEL - 2] + 1
    chosen = jnp.concatenate([jnp.array([0, NCHAN - 1], jnp.int32), middle.astype(jnp.int32)])
    return jax.random.permutation(second_key, chosen)


def setup_inputs(seed: int = 0) -> dict:
    streams_of = jax.random.split(jax.random.key(seed), 3)
    voltages = draw_voltages(jax.random.fold_in(streams_of[2], 71), 0)
    selected = draw_selected(jax.random.fold_in(streams_of[2], 71), 0)
    return dict(voltages=voltages, selected=selected)


def filter_taps():
    position = jnp.arange(TAPS * NFFT, dtype=jnp.float32)
    offset = (position + 0.5) / NFFT - TAPS / 2.0
    hann_part = 0.5 - 0.5 * jnp.cos(2.0 * math.pi * (position + 0.5) / (TAPS * NFFT))
    return (jnp.sinc(offset) * hann_part).reshape(TAPS, NFFT)

def reference(voltages, selected):
    group_size = math.gcd(INPUTS, 64)
    reshaped = voltages.reshape(INPUTS // group_size, group_size, SPECTRA, NFFT)
    window = filter_taps()
    factor = 1.0 / (24.0 * math.sqrt(NFFT))

    def one_group(input_group):
        frames = input_group.astype(jnp.float32)
        padded = jnp.concatenate([jnp.zeros((group_size, TAPS - 1, NFFT), jnp.float32), frames], axis=1)
        summed = jnp.zeros((group_size, SPECTRA, NFFT), jnp.float32)
        for tap_index in range(TAPS):
            summed = summed + window[tap_index][None, None, :] * padded[:, tap_index:tap_index + SPECTRA, :]
        spectrum = jnp.take(jnp.fft.rfft(summed, axis=-1), selected, axis=-1) * factor
        real_part = spectrum.real.astype(jnp.bfloat16)
        imag_part = spectrum.imag.astype(jnp.bfloat16)
        return jnp.stack([real_part, imag_part], axis=0)
    grouped = lax.map(one_group, reshaped)
    spectra = jnp.moveaxis(grouped, 1, 0).reshape(2, INPUTS, SPECTRA, NSEL)
    channel_major = jnp.moveaxis(spectra, 3, 0)

    def one_channel(parts):
        real_part = parts[0]
        imag_part = parts[1]
        real_vis = jnp.dot(real_part, real_part.T, preferred_element_type=jnp.float32) + jnp.dot(imag_part, imag_part.T, preferred_element_type=jnp.float32)
        imag_vis = jnp.dot(imag_part, real_part.T, preferred_element_type=jnp.float32) - jnp.dot(real_part, imag_part.T, preferred_element_type=jnp.float32)
        return jnp.stack([real_vis, imag_vis], axis=0) / SPECTRA
    per_channel = lax.map(one_channel, channel_major)
    return jnp.moveaxis(per_channel, 1, 0)
```

```python
import math

import jax
import jax.numpy as jnp
import numpy as np
from jax import lax
from jax.experimental import pallas as pl
from jax.experimental.pallas import tpu as pltpu
from jax.sharding import Mesh
from jax.sharding import PartitionSpec as P

NFFT = 2048
TAPS = 4
NSEL = 32
LANES = 128
MIB = 1 << 20


def shifted(count, distance):
    return [(i, (i + distance) % count) for i in range(count)]


def filter_taps():
    position = (
        lax.broadcasted_iota(jnp.int32, (8, NFFT), 0) * NFFT
        + lax.broadcasted_iota(jnp.int32, (8, NFFT), 1)
    ).astype(jnp.float32) + 0.5
    turn = math.pi * (position / NFFT - TAPS / 2.0)
    hann_part = 0.5 - 0.5 * jnp.cos(2.0 * math.pi * position / (TAPS * NFFT))
    return jnp.sin(turn) / turn * hann_part


def signed_angle(phase):
    folded = ((phase + NFFT // 2) & (NFFT - 1)) - NFFT // 2
    return folded.astype(jnp.float32) * (2.0 * math.pi / NFFT)


def table_kernel(order, sel_hbm, volt_ref, table_ref, spill_ref, sel_ref, tail_ref, sems):
    reach = tail_ref.shape[2]
    fetch = pltpu.make_async_copy(sel_hbm, sel_ref, sems.at[0])
    fetch.start()
    last = pltpu.make_async_copy(
        volt_ref.at[:, :, pl.ds(volt_ref.shape[2] - reach, reach)], tail_ref, sems.at[1]
    )
    last.start()
    window = filter_taps().T
    fetch.wait()
    lane = lax.broadcasted_iota(jnp.int32, (1, LANES), 1)
    slot = lane & (NSEL - 1)
    sel = jnp.zeros((1, LANES), jnp.int32)
    for position, channel in enumerate(order):
        sel = jnp.where(slot == position, sel_ref[channel], sel)
    quarter = jnp.where((lane & NSEL) != 0, NFFT // 4, 0)
    coarse = lax.broadcasted_iota(jnp.int32, (32, LANES), 0) * 64
    fine = lax.broadcasted_iota(jnp.int32, (64, LANES), 0)
    coarse_angle = signed_angle(coarse * sel)
    fine_angle = signed_angle(fine * sel + quarter)
    coarse_cos, coarse_sin = jnp.cos(coarse_angle), jnp.sin(coarse_angle)
    fine_cos, fine_sin = jnp.cos(fine_angle), jnp.sin(fine_angle)
    upper_lane = lax.broadcasted_iota(jnp.int32, (64, LANES), 1) < LANES // 2
    for a in range(32):
        wave = coarse_cos[a : a + 1, :] * fine_cos - coarse_sin[a : a + 1, :] * fine_sin
        rows = slice(64 * a, 64 * (a + 1))
        for tap in range(TAPS):
            exact = window[rows, tap : tap + 1] * wave
            upper = exact.astype(jnp.bfloat16).astype(jnp.float32)
            table_ref[rows, LANES * tap : LANES * (tap + 1)] = jnp.where(
                upper_lane, upper, exact - upper
            ).astype(jnp.bfloat16)
    last.wait()
    inputs = tail_ref.shape[1]
    product = jnp.dot(
        jnp.concatenate(
            [tail_ref[0, :, NFFT * f : NFFT * (f + 1)] for f in range(TAPS - 1)], axis=0
        ),
        table_ref[...],
        preferred_element_type=jnp.float32,
    )
    for spectrum in range(TAPS - 1):
        total = jnp.zeros((inputs, LANES), jnp.float32)
        for f in range(spectrum, TAPS - 1):
            tap = f - spectrum
            total += product[inputs * f : inputs * (f + 1), LANES * tap : LANES * (tap + 1)]
        spill_ref[inputs * spectrum : inputs * (spectrum + 1), :] = total


def filter_kernel(batch, volt_ref, table_ref, out_ref, held, sems):
    inputs = held.shape[1]
    frames = held.shape[2] // NFFT
    reach = (TAPS - 1) * inputs
    rows = batch * inputs
    copies = []
    for first in range(0, frames, batch):
        part = pl.ds(first * NFFT, batch * NFFT)
        copy = pltpu.make_async_copy(
            volt_ref.at[:, :, part], held.at[:, :, part], sems.at[first // batch]
        )
        copy.start()
        copies.append(copy)
    out_ref[...] = jnp.zeros_like(out_ref)
    for first in range(0, frames, batch):
        copies[first // batch].wait()
        stacked = jnp.concatenate(
            [held[0, :, NFFT * f : NFFT * (f + 1)] for f in range(first, first + batch)], axis=0
        )
        product = jnp.dot(stacked, table_ref[...], preferred_element_type=jnp.float32)
        for tap in range(TAPS):
            start = first * inputs + reach - tap * inputs
            out_ref[start : start + rows, :] += product[:, LANES * tap : LANES * (tap + 1)]


def turn_kernel(spectra, total_ref, halo_ref, out_ref, joined, turned):
    inputs = out_ref.shape[1]
    factor = 1.0 / (24.0 * math.sqrt(NFFT))
    halo_rows = halo_ref.shape[0]
    head = total_ref[0:halo_rows, :] + halo_ref[...]
    body = total_ref[halo_rows : spectra * inputs, :]
    joined[0:halo_rows, :] = (head + pltpu.roll(head, LANES // 2, 1)) * factor
    joined[halo_rows : spectra * inputs, :] = (body + pltpu.roll(body, LANES // 2, 1)) * factor
    low_lane = lax.broadcasted_iota(jnp.int32, (NSEL, LANES), 1) < LANES // 2
    for i in range(0, inputs, 2):
        pair = jnp.concatenate(
            [
                joined[pl.ds(i, spectra, stride=inputs), :],
                joined[pl.ds(i + 1, spectra, stride=inputs), :],
            ],
            axis=0,
        )
        flipped = pair.T
        real, imag = flipped[0:NSEL, :], flipped[NSEL : 2 * NSEL, :]
        turned[pl.ds(i, NSEL, stride=inputs), :] = jnp.where(
            low_lane, real, pltpu.roll(imag, LANES // 2, 1)
        )
        turned[pl.ds(i + 1, NSEL, stride=inputs), :] = jnp.where(
            low_lane, pltpu.roll(real, LANES // 2, 1), imag
        )

    out_ref[...] = turned[...].reshape(NSEL, inputs, LANES).astype(jnp.bfloat16)


def matrix(refs):
    groups, segments = refs[0].shape[:2]
    return jnp.concatenate(
        [
            jnp.concatenate([ref[g, t] for ref in refs for g in range(groups)], axis=0)
            for t in range(segments)
        ],
        axis=1,
    )


def correlate_kernel(scale, count, reach, place_ref, *refs):
    units, out_refs, products = refs[: 2 * count], refs[2 * count : -1], refs[-1]
    sides = 2
    planes = products.shape[0] // sides
    own = matrix(units[0:2])
    low_lane = lax.broadcasted_iota(jnp.int32, (own.shape[0], LANES), 1) < LANES // 2
    swapped = []
    for start in range(0, own.shape[1], LANES):
        rolled = pltpu.roll(own[:, start : start + LANES].astype(jnp.float32), LANES // 2, 1)
        swapped.append(jnp.where(low_lane, rolled, -rolled).astype(jnp.bfloat16))
    left = jnp.concatenate([own, jnp.concatenate(swapped, axis=1)], axis=0)
    span = own.shape[0]
    rows = span // sides
    for u in range(count):
        tile = lax.dot_general(
            left,
            matrix(units[2 * u : 2 * u + 2]),
            (((1,), (1,)), ((), ())),
            preferred_element_type=jnp.float32,
        )
        tile = (tile * scale).astype(jnp.bfloat16)
        origin = place_ref[2 + u]
        column = pl.multiple_of(origin % 2 * span, span)
        for side in range(sides):
            for part in range(2):
                start = span * part + rows * side
                products[planes * side + origin // 2, part, :, pl.ds(column, span)] = tile[
                    start : start + rows, :
                ]
    for (dx, dy), out_ref in zip(reach, out_refs, strict=True):
        side, plane = (place_ref[0] + dx) % sides, (place_ref[1] + dy) % planes
        out_ref[...] = products[planes * side + plane]


def widen_kernel(count, place_ref, *refs):
    pieces, out_ref, wide, sems = refs[:count], refs[count], refs[count + 1], refs[count + 2]
    copies = []
    for k in range(count):
        channel = place_ref[k]
        for part in range(2):
            wide[k, part] = pieces[k][part].astype(jnp.float32)
            copy = pltpu.make_async_copy(
                wide.at[k, part], out_ref.at[part, channel], sems.at[k, part]
            )
            copy.start()
            copies.append(copy)
    for copy in copies:
        copy.wait()


def vmem(count=1):
    return [pl.BlockSpec(memory_space=pltpu.VMEM)] * count


def smem():
    return pl.BlockSpec(memory_space=pltpu.SMEM)


def body(voltages, selected):
    inputs = voltages.shape[1]
    spectra = voltages.shape[2] // NFFT
    segments = lax.axis_size("y")
    sides = lax.axis_size("xhi")
    ring = lax.axis_size("z")
    here_z, here_x, here_y = (lax.axis_index(a) for a in ("z", "xhi", "y"))

    order = np.arange(NSEL).reshape(2, 2, 2, 4).transpose(2, 0, 1, 3).reshape(-1)
    tables, spill = pl.pallas_call(
        lambda *refs: table_kernel([int(c) for c in order], *refs),
        in_specs=[pl.BlockSpec(memory_space=pl.ANY)] * 2,
        out_specs=vmem(2),
        out_shape=[
            jax.ShapeDtypeStruct((NFFT, TAPS * LANES), jnp.bfloat16),
            jax.ShapeDtypeStruct(((TAPS - 1) * inputs, LANES), jnp.float32),
        ],
        scratch_shapes=[
            pltpu.SMEM((NSEL,), jnp.int32),
            pltpu.VMEM((1, inputs, (TAPS - 1) * NFFT), jnp.bfloat16),
            pltpu.SemaphoreType.DMA((2,)),
        ],
        compiler_params=pltpu.CompilerParams(vmem_limit_bytes=46 * MIB),
        name="tables",
    )(selected, voltages)
    halo = lax.ppermute(spill, "y", [(i, i + 1) for i in range(segments - 1)])

    batch = 16
    filtered = pl.pallas_call(
        lambda *refs: filter_kernel(batch, *refs),
        in_specs=[pl.BlockSpec(memory_space=pl.ANY)] + vmem(),
        out_specs=vmem()[0],
        out_shape=jax.ShapeDtypeStruct(((spectra + TAPS - 1) * inputs, LANES), jnp.float32),
        scratch_shapes=[
            pltpu.VMEM(voltages.shape, voltages.dtype),
            pltpu.SemaphoreType.DMA((spectra // batch,)),
        ],
        compiler_params=pltpu.CompilerParams(vmem_limit_bytes=46 * MIB),
        cost_estimate=pl.CostEstimate(
            flops=2 * spectra * inputs * NFFT * TAPS * LANES,
            bytes_accessed=12 * MIB,
            transcendentals=0,
        ),
        name="filter_bank",
    )(voltages, tables)

    spectrum = pl.pallas_call(
        lambda *refs: turn_kernel(spectra, *refs),
        in_specs=vmem(2),
        out_specs=vmem()[0],
        out_shape=jax.ShapeDtypeStruct((NSEL, inputs, LANES), jnp.bfloat16),
        scratch_shapes=[
            pltpu.VMEM((spectra * inputs, LANES), jnp.float32),
            pltpu.VMEM((NSEL * inputs, LANES), jnp.float32),
        ],
        compiler_params=pltpu.CompilerParams(vmem_limit_bytes=8 * MIB),
        name="turn",
    )(filtered, halo)

    arrived = lax.all_to_all(
        spectrum, ("xhi", "xlo", "core", "y"), split_axis=0, concat_axis=0, tiled=True
    )
    own = arrived.reshape(8, segments, inputs, LANES)

    half = own.shape[0] // 2
    low, high = own[:half], own[half:]
    units = [low, high]
    right_low = left_low = low
    right_high = left_high = high
    for _ in range(ring // 2 - 1):
        right_low = lax.ppermute(right_low, "z", shifted(ring, 1))
        left_high = lax.ppermute(left_high, "z", shifted(ring, -1))
        right_high = lax.ppermute(right_high, "z", shifted(ring, 1))
        left_low = lax.ppermute(left_low, "z", shifted(ring, -1))
        units += [right_low, right_high, left_low, left_high]
    units.append(lax.ppermute(right_low, "z", shifted(ring, 1)))
    units.append(lax.ppermute(left_high, "z", shifted(ring, -1)))
    offsets = [0]
    for d in range(1, ring // 2):
        offsets += [-d, d]
    offsets.append(ring // 2)
    origin = [(here_z + d) % ring for d in offsets]

    scale = 1.0 / (spectra * segments)
    rows = half * inputs
    reach = ((1, 2), (0, 2), (1, 1), (1, 3), (0, 1), (0, 3), (1, 0), (0, 0))
    place = jnp.stack([here_x, here_y] + origin).astype(jnp.int32)
    products = pl.pallas_call(
        lambda *refs: correlate_kernel(scale, len(origin), reach, *refs),
        in_specs=[smem()] + vmem(len(units)),
        out_specs=vmem(len(reach)),
        out_shape=[jax.ShapeDtypeStruct((2, rows, 4 * rows), jnp.bfloat16)] * len(reach),
        scratch_shapes=[pltpu.VMEM((len(reach), 2, rows, 4 * rows), jnp.bfloat16)],
        compiler_params=pltpu.CompilerParams(vmem_limit_bytes=12 * MIB),
        name="correlate",
    )(place, *units)
    pieces, channels = [], []
    for (dx, dy), product in zip(reach, products, strict=True):
        if dx or dy:
            route = [
                (x * segments + y, (x + dx) % sides * segments + (y + dy) % segments)
                for x in range(sides)
                for y in range(segments)
            ]
            product = lax.ppermute(product, ("xhi", "y"), route)
        pieces.append(product)
        channels.append((here_x - dx) % sides * segments + (here_y - dy) % segments)

    return pl.pallas_call(
        lambda *refs: widen_kernel(len(pieces), *refs),
        in_specs=[smem()] + vmem(len(pieces)),
        out_specs=pl.BlockSpec(memory_space=pl.ANY),
        out_shape=jax.ShapeDtypeStruct((2, len(pieces), rows, 4 * rows), jnp.float32),
        scratch_shapes=[
            pltpu.VMEM((len(pieces), 2, rows, 4 * rows), jnp.float32),
            pltpu.SemaphoreType.DMA((len(pieces), 2)),
        ],
        compiler_params=pltpu.CompilerParams(vmem_limit_bytes=10 * MIB),
        name="widen",
    )(jnp.stack(channels).astype(jnp.int32), *pieces)


def solution(mesh):
    fine = Mesh(mesh.devices.reshape(2, 2, 8, 2, 4), ("xlo", "core", "z", "xhi", "y"))
    return jax.shard_map(
        body,
        mesh=fine,
        in_specs=(P(("z", "xhi"), ("xlo", "core"), "y"), P()),
        out_specs=P(None, ("xlo", "core"), ("z", "xhi"), "y"),
        check_vma=False,
    )
```

```python
import math

import jax
import jax.numpy as jnp
import numpy as np
from jax import lax
from jax.experimental import pallas as pl
from jax.experimental.pallas import tpu as pltpu
from jax.sharding import Mesh
from jax.sharding import PartitionSpec as P

NFFT = 2048
TAPS = 4
NSEL = 32
LANES = 128
MIB = 1 << 20


def shifted(count, distance):
    return [(i, (i + distance) % count) for i in range(count)]


def filter_taps():
    position = (
        lax.broadcasted_iota(jnp.int32, (8, NFFT), 0) * NFFT
        + lax.broadcasted_iota(jnp.int32, (8, NFFT), 1)
    ).astype(jnp.float32) + 0.5
    turn = math.pi * (position / NFFT - TAPS / 2.0)
    hann_part = 0.5 - 0.5 * jnp.cos(2.0 * math.pi * position / (TAPS * NFFT))
    return jnp.sin(turn) / turn * hann_part


def signed_angle(phase):
    folded = ((phase + NFFT // 2) & (NFFT - 1)) - NFFT // 2
    return folded.astype(jnp.float32) * (2.0 * math.pi / NFFT)


def table_kernel(order, sel_hbm, volt_ref, table_ref, spill_ref, held_ref, sel_ref, sems):
    chunks = sems.shape[0] - 1
    fetch = pltpu.make_async_copy(sel_hbm, sel_ref, sems.at[chunks])
    fetch.start()
    width = volt_ref.shape[2] // chunks
    copies = []
    for c in reversed(range(chunks)):
        part = pl.ds(c * width, width)
        copy = pltpu.make_async_copy(volt_ref.at[:, :, part], held_ref.at[:, :, part], sems.at[c])
        copy.start()
        copies.append(copy)
    window = filter_taps().T
    fetch.wait()
    lane = lax.broadcasted_iota(jnp.int32, (1, LANES), 1)
    slot = lane & (NSEL - 1)
    sel = jnp.zeros((1, LANES), jnp.int32)
    for position, channel in enumerate(order):
        sel = jnp.where(slot == position, sel_ref[channel], sel)
    quarter = jnp.where((lane & NSEL) != 0, NFFT // 4, 0)
    coarse = lax.broadcasted_iota(jnp.int32, (32, LANES), 0) * 64
    fine = lax.broadcasted_iota(jnp.int32, (64, LANES), 0)
    coarse_angle = signed_angle(coarse * sel)
    fine_angle = signed_angle(fine * sel + quarter)
    coarse_cos, coarse_sin = jnp.cos(coarse_angle), jnp.sin(coarse_angle)
    fine_cos, fine_sin = jnp.cos(fine_angle), jnp.sin(fine_angle)
    upper_lane = lax.broadcasted_iota(jnp.int32, (64, LANES), 1) < LANES // 2
    for a in range(32):
        wave = coarse_cos[a : a + 1, :] * fine_cos - coarse_sin[a : a + 1, :] * fine_sin
        rows = slice(64 * a, 64 * (a + 1))
        for tap in range(TAPS):
            exact = window[rows, tap : tap + 1] * wave
            upper = exact.astype(jnp.bfloat16).astype(jnp.float32)
            table_ref[rows, LANES * tap : LANES * (tap + 1)] = jnp.where(
                upper_lane, upper, exact - upper
            ).astype(jnp.bfloat16)
    copies[0].wait()
    inputs = held_ref.shape[1]
    frames = held_ref.shape[2] // NFFT
    tail = range(frames - TAPS + 1, frames)
    product = jnp.dot(
        jnp.concatenate([held_ref[0, :, NFFT * f : NFFT * (f + 1)] for f in tail], axis=0),
        table_ref[...],
        preferred_element_type=jnp.float32,
    )
    for spectrum in range(TAPS - 1):
        total = jnp.zeros((inputs, LANES), jnp.float32)
        for f in range(spectrum, TAPS - 1):
            tap = f - spectrum
            total += product[inputs * f : inputs * (f + 1), LANES * tap : LANES * (tap + 1)]
        spill_ref[inputs * spectrum : inputs * (spectrum + 1), :] = total
    for copy in copies[1:]:
        copy.wait()


def filter_kernel(batch, volt_ref, table_ref, out_ref):
    inputs = volt_ref.shape[1]
    frames = volt_ref.shape[2] // NFFT
    reach = (TAPS - 1) * inputs
    rows = batch * inputs
    out_ref[...] = jnp.zeros_like(out_ref)
    for first in range(0, frames, batch):
        stacked = jnp.concatenate(
            [volt_ref[0, :, NFFT * f : NFFT * (f + 1)] for f in range(first, first + batch)], axis=0
        )
        product = jnp.dot(stacked, table_ref[...], preferred_element_type=jnp.float32)
        for tap in range(TAPS):
            start = first * inputs + reach - tap * inputs
            out_ref[start : start + rows, :] += product[:, LANES * tap : LANES * (tap + 1)]


def turn_kernel(spectra, total_ref, halo_ref, out_ref, joined, turned):
    inputs = out_ref.shape[1]
    factor = 1.0 / (24.0 * math.sqrt(NFFT))
    halo_rows = halo_ref.shape[0]
    head = total_ref[0:halo_rows, :] + halo_ref[...]
    body = total_ref[halo_rows : spectra * inputs, :]
    joined[0:halo_rows, :] = (head + pltpu.roll(head, LANES // 2, 1)) * factor
    joined[halo_rows : spectra * inputs, :] = (body + pltpu.roll(body, LANES // 2, 1)) * factor
    low_lane = lax.broadcasted_iota(jnp.int32, (NSEL, LANES), 1) < LANES // 2
    for i in range(0, inputs, 2):
        pair = jnp.concatenate(
            [
                joined[pl.ds(i, spectra, stride=inputs), :],
                joined[pl.ds(i + 1, spectra, stride=inputs), :],
            ],
            axis=0,
        )
        flipped = pair.T
        real, imag = flipped[0:NSEL, :], flipped[NSEL : 2 * NSEL, :]
        turned[pl.ds(i, NSEL, stride=inputs), :] = jnp.where(
            low_lane, real, pltpu.roll(imag, LANES // 2, 1)
        )
        turned[pl.ds(i + 1, NSEL, stride=inputs), :] = jnp.where(
            low_lane, pltpu.roll(real, LANES // 2, 1), imag
        )

    out_ref[...] = turned[...].reshape(NSEL, inputs, LANES).astype(jnp.bfloat16)


def matrix(refs):
    groups, segments = refs[0].shape[:2]
    return jnp.concatenate(
        [
            jnp.concatenate([ref[g, t] for ref in refs for g in range(groups)], axis=0)
            for t in range(segments)
        ],
        axis=1,
    )


def own_rows(refs):
    own = matrix(refs)
    low_lane = lax.broadcasted_iota(jnp.int32, (own.shape[0], LANES), 1) < LANES // 2
    swapped = []
    for start in range(0, own.shape[1], LANES):
        rolled = pltpu.roll(own[:, start : start + LANES].astype(jnp.float32), LANES // 2, 1)
        swapped.append(jnp.where(low_lane, rolled, -rolled).astype(jnp.bfloat16))
    return jnp.concatenate([own, jnp.concatenate(swapped, axis=1)], axis=0)


def tile_of(left, refs, scale):
    tile = lax.dot_general(
        left, matrix(refs), (((1,), (1,)), ((), ())), preferred_element_type=jnp.float32
    )
    return (tile * scale).astype(jnp.bfloat16)


def near_kernel(scale, ring, offsets, split, here_ref, *refs):
    units, products_ref, left_ref = refs[:-2], refs[-2], refs[-1]
    planes = products_ref.shape[0] // 2
    left_ref[...] = own_rows(units[: split[0]])
    span = left_ref.shape[0] // 2
    rows = span // 2
    taken = 0
    for offset, count in zip(offsets, split, strict=True):
        tile = tile_of(left_ref[...], units[taken : taken + count], scale)
        taken += count
        origin = lax.rem(here_ref[0] + offset + ring, ring)
        column = pl.multiple_of(origin % 2 * span, span)
        for side in range(2):
            for part in range(2):
                start = span * part + rows * side
                products_ref[planes * side + origin // 2, part, :, pl.ds(column, span)] = tile[
                    start : start + rows, :
                ]


def far_kernel(scale, ring, reach, count, here_ref, products_ref, left_ref, *refs):
    units, out_refs = refs[:count], refs[count:]
    planes = products_ref.shape[0] // 2
    tile = tile_of(left_ref[...], units, scale)
    span = left_ref.shape[0] // 2
    rows = span // 2
    origin = lax.rem(here_ref[0] + ring // 2, ring)
    column = pl.multiple_of(origin % 2 * span, span)
    for (dx, dy), out_ref in zip(reach, out_refs, strict=True):
        side, plane = lax.rem(here_ref[1] + dx, 2), lax.rem(here_ref[2] + dy, planes)
        out_ref[...] = products_ref[planes * side + plane]

        @pl.when(plane == origin // 2)
        def _(side=side, out_ref=out_ref):
            for part in range(2):
                upper = tile[span * part : span * part + rows, :]
                lower = tile[span * part + rows : span * (part + 1), :]
                out_ref[part, :, pl.ds(column, span)] = jnp.where(side == 0, upper, lower)


def store_kernel(reach, here_ref, *refs):
    count = len(reach)
    pieces, out_ref, wide, sems = refs[:count], refs[-3], refs[-2], refs[-1]
    copies = []
    for k, (dx, dy) in enumerate(reach):
        channel = 4 * lax.rem(here_ref[1] + 2 - dx, 2) + lax.rem(here_ref[2] + 4 - dy, 4)
        for part in range(2):
            wide[k, part] = pieces[k][part].astype(jnp.float32)
            copy = pltpu.make_async_copy(
                wide.at[k, part], out_ref.at[part, channel], sems.at[k, part]
            )
            copy.start()
            copies.append(copy)
    for copy in copies:
        copy.wait()


def vmem(count=1):
    return [pl.BlockSpec(memory_space=pltpu.VMEM)] * count


def smem():
    return pl.BlockSpec(memory_space=pltpu.SMEM)


def body(voltages, selected):
    inputs = voltages.shape[1]
    spectra = voltages.shape[2] // NFFT
    segments = lax.axis_size("y")
    sides = lax.axis_size("xhi")
    ring = lax.axis_size("z")
    here = jnp.stack([lax.axis_index(a) for a in ("z", "xhi", "y")]).astype(jnp.int32)
    here, selected = lax.optimization_barrier((here, selected))

    order = np.arange(NSEL).reshape(2, 2, 2, 4).transpose(2, 0, 1, 3).reshape(-1)
    tables, spill, held = pl.pallas_call(
        lambda *refs: table_kernel([int(c) for c in order], *refs),
        in_specs=[pl.BlockSpec(memory_space=pl.ANY)] * 2,
        out_specs=vmem(3),
        out_shape=[
            jax.ShapeDtypeStruct((NFFT, TAPS * LANES), jnp.bfloat16),
            jax.ShapeDtypeStruct(((TAPS - 1) * inputs, LANES), jnp.float32),
            jax.ShapeDtypeStruct(voltages.shape, voltages.dtype),
        ],
        scratch_shapes=[
            pltpu.SMEM((NSEL,), jnp.int32),
            pltpu.SemaphoreType.DMA((9,)),
        ],
        compiler_params=pltpu.CompilerParams(vmem_limit_bytes=40 * MIB),
        name="tables",
    )(selected, voltages)
    halo = lax.ppermute(spill, "y", [(i, i + 1) for i in range(segments - 1)])

    filtered = pl.pallas_call(
        lambda *refs: filter_kernel(16, *refs),
        in_specs=vmem(2),
        out_specs=vmem()[0],
        out_shape=jax.ShapeDtypeStruct(((spectra + TAPS - 1) * inputs, LANES), jnp.float32),
        compiler_params=pltpu.CompilerParams(vmem_limit_bytes=20 * MIB),
        cost_estimate=pl.CostEstimate(
            flops=2 * spectra * inputs * NFFT * TAPS * LANES,
            bytes_accessed=12 * MIB,
            transcendentals=0,
        ),
        name="filter_bank",
    )(held, tables)

    spectrum = pl.pallas_call(
        lambda *refs: turn_kernel(spectra, *refs),
        in_specs=vmem(2),
        out_specs=vmem()[0],
        out_shape=jax.ShapeDtypeStruct((NSEL, inputs, LANES), jnp.bfloat16),
        scratch_shapes=[
            pltpu.VMEM((spectra * inputs, LANES), jnp.float32),
            pltpu.VMEM((NSEL * inputs, LANES), jnp.float32),
        ],
        compiler_params=pltpu.CompilerParams(vmem_limit_bytes=8 * MIB),
        name="turn",
    )(filtered, halo)

    arrived = lax.all_to_all(
        spectrum, ("xhi", "xlo", "core", "y"), split_axis=0, concat_axis=0, tiled=True
    )
    own = arrived.reshape(8, segments, inputs, LANES)

    half = own.shape[0] // 2
    low, high = own[:half], own[half:]
    near = [low, high]
    right_low = left_low = low
    right_high = left_high = high
    offsets = [0]
    for step in range(1, ring // 2):
        right_low = lax.ppermute(right_low, "z", shifted(ring, 1))
        left_high = lax.ppermute(left_high, "z", shifted(ring, -1))
        right_high = lax.ppermute(right_high, "z", shifted(ring, 1))
        left_low = lax.ppermute(left_low, "z", shifted(ring, -1))
        near += [right_low, right_high, left_low, left_high]
        offsets += [-step, step]
    split = (2,) * len(offsets)
    far = [
        lax.ppermute(right_low, "z", shifted(ring, 1)),
        lax.ppermute(left_high, "z", shifted(ring, -1)),
    ]
    scale = 1.0 / (spectra * segments)
    rows = half * inputs
    reach = ((1, 2), (0, 2), (1, 1), (1, 3), (0, 1), (0, 3), (1, 0), (0, 0))
    piece = jax.ShapeDtypeStruct((2, rows, 4 * rows), jnp.bfloat16)
    products, left = pl.pallas_call(
        lambda *refs: near_kernel(scale, ring, offsets, split, *refs),
        in_specs=[smem()] + vmem(len(near)),
        out_specs=vmem(2),
        out_shape=[
            jax.ShapeDtypeStruct((len(reach), *piece.shape), jnp.bfloat16),
            jax.ShapeDtypeStruct((4 * rows, segments * LANES), jnp.bfloat16),
        ],
        compiler_params=pltpu.CompilerParams(vmem_limit_bytes=10 * MIB),
        cost_estimate=pl.CostEstimate(
            flops=2 * len(offsets) * 4 * rows * 2 * rows * segments * LANES,
            bytes_accessed=4 * MIB,
            transcendentals=0,
        ),
        name="near",
    )(here, *near)
    shares = pl.pallas_call(
        lambda *refs: far_kernel(scale, ring, reach, len(far), *refs),
        in_specs=[smem()] + vmem(2 + len(far)),
        out_specs=vmem(len(reach)),
        out_shape=[piece] * len(reach),
        compiler_params=pltpu.CompilerParams(vmem_limit_bytes=10 * MIB),
        name="far",
    )(here, products, left, *far)
    pieces = []
    for (dx, dy), share in zip(reach, shares, strict=True):
        if dx or dy:
            route = [
                (x * segments + y, (x + dx) % sides * segments + (y + dy) % segments)
                for x in range(sides)
                for y in range(segments)
            ]
            share = lax.ppermute(share, ("xhi", "y"), route)
        pieces.append(share)

    def store(numbers, before):
        return pl.pallas_call(
            lambda *refs: store_kernel([reach[k] for k in numbers], *refs),
            in_specs=[smem()]
            + vmem(len(numbers))
            + [pl.BlockSpec(memory_space=pl.ANY)] * len(before),
            out_specs=pl.BlockSpec(memory_space=pl.ANY),
            out_shape=jax.ShapeDtypeStruct((2, len(reach), rows, 4 * rows), jnp.float32),
            scratch_shapes=[
                pltpu.VMEM((len(numbers), 2, rows, 4 * rows), jnp.float32),
                pltpu.SemaphoreType.DMA((len(numbers), 2)),
            ],
            input_output_aliases={1 + len(numbers): 0} if before else {},
            compiler_params=pltpu.CompilerParams(vmem_limit_bytes=10 * MIB),
            name="store",
        )(here, *[pieces[k] for k in numbers], *before)

    return store((4, 5, 6), (store((7, 0, 1, 2, 3), ()),))


def solution(mesh):
    fine = Mesh(mesh.devices.reshape(2, 2, 8, 2, 4), ("xlo", "core", "z", "xhi", "y"))
    return jax.shard_map(
        body,
        mesh=fine,
        in_specs=(P(("z", "xhi"), ("xlo", "core"), "y"), P()),
        out_specs=P(None, ("xlo", "core"), ("z", "xhi"), "y"),
        check_vma=False,
    )
```

```python
import math

import jax
import jax.numpy as jnp
import numpy as np
from jax import lax
from jax.experimental import pallas as pl
from jax.experimental.pallas import tpu as pltpu
from jax.sharding import Mesh
from jax.sharding import PartitionSpec as P

NFFT = 2048
TAPS = 4
NSEL = 32
LANES = 128
MIB = 1 << 20


def shifted(count, distance):
    return [(i, (i + distance) % count) for i in range(count)]


def filter_taps():
    position = (
        lax.broadcasted_iota(jnp.int32, (8, NFFT), 0) * NFFT
        + lax.broadcasted_iota(jnp.int32, (8, NFFT), 1)
    ).astype(jnp.float32) + 0.5
    turn = math.pi * (position / NFFT - TAPS / 2.0)
    hann_part = 0.5 - 0.5 * jnp.cos(2.0 * math.pi * position / (TAPS * NFFT))
    return jnp.sin(turn) / turn * hann_part


def signed_angle(phase):
    folded = ((phase + NFFT // 2) & (NFFT - 1)) - NFFT // 2
    return folded.astype(jnp.float32) * (2.0 * math.pi / NFFT)


def table_kernel(order, sel_hbm, volt_ref, table_ref, spill_ref, held_ref, sel_ref, sems):
    chunks = sems.shape[0] - 1
    fetch = pltpu.make_async_copy(sel_hbm, sel_ref, sems.at[chunks])
    fetch.start()
    width = volt_ref.shape[2] // chunks
    copies = []
    for c in reversed(range(chunks)):
        part = pl.ds(c * width, width)
        copy = pltpu.make_async_copy(volt_ref.at[:, :, part], held_ref.at[:, :, part], sems.at[c])
        copy.start()
        copies.append(copy)
    window = filter_taps().T
    fetch.wait()
    lane = lax.broadcasted_iota(jnp.int32, (1, LANES), 1)
    slot = lane & (NSEL - 1)
    sel = jnp.zeros((1, LANES), jnp.int32)
    for position, channel in enumerate(order):
        sel = jnp.where(slot == position, sel_ref[channel], sel)
    quarter = jnp.where((lane & NSEL) != 0, NFFT // 4, 0)
    coarse = lax.broadcasted_iota(jnp.int32, (32, LANES), 0) * 64
    fine = lax.broadcasted_iota(jnp.int32, (64, LANES), 0)
    coarse_angle = signed_angle(coarse * sel)
    fine_angle = signed_angle(fine * sel + quarter)
    coarse_cos, coarse_sin = jnp.cos(coarse_angle), jnp.sin(coarse_angle)
    fine_cos, fine_sin = jnp.cos(fine_angle), jnp.sin(fine_angle)
    upper_lane = lax.broadcasted_iota(jnp.int32, (64, LANES), 1) < LANES // 2
    for a in range(32):
        wave = coarse_cos[a : a + 1, :] * fine_cos - coarse_sin[a : a + 1, :] * fine_sin
        rows = slice(64 * a, 64 * (a + 1))
        for tap in range(TAPS):
            exact = window[rows, tap : tap + 1] * wave
            upper = exact.astype(jnp.bfloat16).astype(jnp.float32)
            table_ref[rows, LANES * tap : LANES * (tap + 1)] = jnp.where(
                upper_lane, upper, exact - upper
            ).astype(jnp.bfloat16)
    copies[0].wait()
    inputs = held_ref.shape[1]
    frames = held_ref.shape[2] // NFFT
    tail = range(frames - TAPS + 1, frames)
    product = jnp.dot(
        jnp.concatenate([held_ref[0, :, NFFT * f : NFFT * (f + 1)] for f in tail], axis=0),
        table_ref[...],
        preferred_element_type=jnp.float32,
    )
    for spectrum in range(TAPS - 1):
        total = jnp.zeros((inputs, LANES), jnp.float32)
        for f in range(spectrum, TAPS - 1):
            tap = f - spectrum
            total += product[inputs * f : inputs * (f + 1), LANES * tap : LANES * (tap + 1)]
        spill_ref[inputs * spectrum : inputs * (spectrum + 1), :] = total
    for copy in copies[1:]:
        copy.wait()


def filter_kernel(batch, volt_ref, table_ref, out_ref):
    inputs = volt_ref.shape[1]
    frames = volt_ref.shape[2] // NFFT
    reach = (TAPS - 1) * inputs
    rows = batch * inputs
    out_ref[...] = jnp.zeros_like(out_ref)
    for first in range(0, frames, batch):
        stacked = jnp.concatenate(
            [volt_ref[0, :, NFFT * f : NFFT * (f + 1)] for f in range(first, first + batch)], axis=0
        )
        product = jnp.dot(stacked, table_ref[...], preferred_element_type=jnp.float32)
        for tap in range(TAPS):
            start = first * inputs + reach - tap * inputs
            out_ref[start : start + rows, :] += product[:, LANES * tap : LANES * (tap + 1)]


def turn_kernel(spectra, total_ref, halo_ref, out_ref, joined, turned):
    inputs = out_ref.shape[1]
    factor = 1.0 / (24.0 * math.sqrt(NFFT))
    halo_rows = halo_ref.shape[0]
    head = total_ref[0:halo_rows, :] + halo_ref[...]
    body = total_ref[halo_rows : spectra * inputs, :]
    joined[0:halo_rows, :] = (head + pltpu.roll(head, LANES // 2, 1)) * factor
    joined[halo_rows : spectra * inputs, :] = (body + pltpu.roll(body, LANES // 2, 1)) * factor
    low_lane = lax.broadcasted_iota(jnp.int32, (NSEL, LANES), 1) < LANES // 2
    for i in range(0, inputs, 2):
        pair = jnp.concatenate(
            [
                joined[pl.ds(i, spectra, stride=inputs), :],
                joined[pl.ds(i + 1, spectra, stride=inputs), :],
            ],
            axis=0,
        )
        flipped = pair.T
        real, imag = flipped[0:NSEL, :], flipped[NSEL : 2 * NSEL, :]
        turned[pl.ds(i, NSEL, stride=inputs), :] = jnp.where(
            low_lane, real, pltpu.roll(imag, LANES // 2, 1)
        )
        turned[pl.ds(i + 1, NSEL, stride=inputs), :] = jnp.where(
            low_lane, pltpu.roll(real, LANES // 2, 1), imag
        )

    out_ref[...] = turned[...].reshape(NSEL, inputs, LANES).astype(jnp.bfloat16)


def matrix(refs):
    groups, segments = refs[0].shape[:2]
    return jnp.concatenate(
        [
            jnp.concatenate([ref[g, t] for ref in refs for g in range(groups)], axis=0)
            for t in range(segments)
        ],
        axis=1,
    )


def own_rows(refs):
    own = matrix(refs)
    low_lane = lax.broadcasted_iota(jnp.int32, (own.shape[0], LANES), 1) < LANES // 2
    swapped = []
    for start in range(0, own.shape[1], LANES):
        rolled = pltpu.roll(own[:, start : start + LANES].astype(jnp.float32), LANES // 2, 1)
        swapped.append(jnp.where(low_lane, rolled, -rolled).astype(jnp.bfloat16))
    return jnp.concatenate([own, jnp.concatenate(swapped, axis=1)], axis=0)


def tile_of(left, refs, scale):
    tile = lax.dot_general(
        left, matrix(refs), (((1,), (1,)), ((), ())), preferred_element_type=jnp.float32
    )
    return (tile * scale).astype(jnp.bfloat16)


def near_kernel(scale, ring, offsets, split, here_ref, *refs):
    units, products_ref, left_ref = refs[:-2], refs[-2], refs[-1]
    planes = products_ref.shape[0] // 2
    left_ref[...] = own_rows(units[: split[0]])
    span = left_ref.shape[0] // 2
    rows = span // 2
    taken = 0
    for offset, count in zip(offsets, split, strict=True):
        tile = tile_of(left_ref[...], units[taken : taken + count], scale)
        taken += count
        origin = lax.rem(here_ref[0] + offset + ring, ring)
        column = pl.multiple_of(origin % 2 * span, span)
        for side in range(2):
            for part in range(2):
                start = span * part + rows * side
                products_ref[planes * side + origin // 2, part, :, pl.ds(column, span)] = tile[
                    start : start + rows, :
                ]


def far_kernel(scale, ring, reach, count, here_ref, products_ref, left_ref, *refs):
    units, out_refs = refs[:count], refs[count:]
    planes = products_ref.shape[0] // 2
    tile = tile_of(left_ref[...], units, scale)
    span = left_ref.shape[0] // 2
    rows = span // 2
    origin = lax.rem(here_ref[0] + ring // 2, ring)
    column = pl.multiple_of(origin % 2 * span, span)
    for (dx, dy), out_ref in zip(reach, out_refs, strict=True):
        side, plane = lax.rem(here_ref[1] + dx, 2), lax.rem(here_ref[2] + dy, planes)
        out_ref[...] = products_ref[planes * side + plane]

        @pl.when(plane == origin // 2)
        def _(side=side, out_ref=out_ref):
            for part in range(2):
                upper = tile[span * part : span * part + rows, :]
                lower = tile[span * part + rows : span * (part + 1), :]
                out_ref[part, :, pl.ds(column, span)] = jnp.where(side == 0, upper, lower)


def store_kernel(reach, here_ref, *refs):
    count = len(reach)
    pieces, out_ref, wide, sems = refs[:count], refs[-3], refs[-2], refs[-1]
    copies = []
    for k, (dx, dy) in enumerate(reach):
        channel = 4 * lax.rem(here_ref[1] + 2 - dx, 2) + lax.rem(here_ref[2] + 4 - dy, 4)
        for part in range(2):
            wide[k, part] = pieces[k][part].astype(jnp.float32)
            copy = pltpu.make_async_copy(
                wide.at[k, part], out_ref.at[part, channel], sems.at[k, part]
            )
            copy.start()
            copies.append(copy)
    for copy in copies:
        copy.wait()


def vmem(count=1):
    return [pl.BlockSpec(memory_space=pltpu.VMEM)] * count


def smem():
    return pl.BlockSpec(memory_space=pltpu.SMEM)


def body(voltages, selected):
    inputs = voltages.shape[1]
    spectra = voltages.shape[2] // NFFT
    segments = lax.axis_size("y")
    sides = lax.axis_size("xhi")
    ring = lax.axis_size("z")
    here = jnp.stack([lax.axis_index(a) for a in ("z", "xhi", "y")]).astype(jnp.int32)
    here, selected = lax.optimization_barrier((here, selected))

    order = np.arange(NSEL).reshape(2, 2, 2, 4).transpose(2, 0, 1, 3).reshape(-1)
    tables, spill, held = pl.pallas_call(
        lambda *refs: table_kernel([int(c) for c in order], *refs),
        in_specs=[pl.BlockSpec(memory_space=pl.ANY)] * 2,
        out_specs=vmem(3),
        out_shape=[
            jax.ShapeDtypeStruct((NFFT, TAPS * LANES), jnp.bfloat16),
            jax.ShapeDtypeStruct(((TAPS - 1) * inputs, LANES), jnp.float32),
            jax.ShapeDtypeStruct(voltages.shape, voltages.dtype),
        ],
        scratch_shapes=[
            pltpu.SMEM((NSEL,), jnp.int32),
            pltpu.SemaphoreType.DMA((9,)),
        ],
        compiler_params=pltpu.CompilerParams(vmem_limit_bytes=40 * MIB),
        name="tables",
    )(selected, voltages)
    halo = lax.ppermute(spill, "y", [(i, i + 1) for i in range(segments - 1)])

    filtered = pl.pallas_call(
        lambda *refs: filter_kernel(16, *refs),
        in_specs=vmem(2),
        out_specs=vmem()[0],
        out_shape=jax.ShapeDtypeStruct(((spectra + TAPS - 1) * inputs, LANES), jnp.float32),
        compiler_params=pltpu.CompilerParams(vmem_limit_bytes=20 * MIB),
        cost_estimate=pl.CostEstimate(
            flops=2 * spectra * inputs * NFFT * TAPS * LANES,
            bytes_accessed=12 * MIB,
            transcendentals=0,
        ),
        name="filter_bank",
    )(held, tables)

    spectrum = pl.pallas_call(
        lambda *refs: turn_kernel(spectra, *refs),
        in_specs=vmem(2),
        out_specs=vmem()[0],
        out_shape=jax.ShapeDtypeStruct((NSEL, inputs, LANES), jnp.bfloat16),
        scratch_shapes=[
            pltpu.VMEM((spectra * inputs, LANES), jnp.float32),
            pltpu.VMEM((NSEL * inputs, LANES), jnp.float32),
        ],
        compiler_params=pltpu.CompilerParams(vmem_limit_bytes=8 * MIB),
        name="turn",
    )(filtered, halo)

    arrived = lax.all_to_all(
        spectrum, ("xhi", "xlo", "core", "y"), split_axis=0, concat_axis=0, tiled=True
    )
    own = arrived.reshape(8, segments, inputs, LANES)

    half = own.shape[0] // 2
    low, high = own[:half], own[half:]
    near = [low, high]
    right_low = left_low = low
    right_high = left_high = high
    offsets = [0]
    for step in range(1, ring // 2):
        right_low = lax.ppermute(right_low, "z", shifted(ring, 1))
        left_high = lax.ppermute(left_high, "z", shifted(ring, -1))
        right_high = lax.ppermute(right_high, "z", shifted(ring, 1))
        left_low = lax.ppermute(left_low, "z", shifted(ring, -1))
        near += [right_low, right_high, left_low, left_high]
        offsets += [-step, step]
    split = (2,) * len(offsets)
    far = [
        lax.ppermute(right_low, "z", shifted(ring, 1)),
        lax.ppermute(left_high, "z", shifted(ring, -1)),
    ]
    scale = 1.0 / (spectra * segments)
    rows = half * inputs
    reach = ((1, 2), (1, 1), (1, 3), (0, 2), (1, 0), (0, 1), (0, 3), (0, 0))
    piece = jax.ShapeDtypeStruct((2, rows, 4 * rows), jnp.bfloat16)
    products, left = pl.pallas_call(
        lambda *refs: near_kernel(scale, ring, offsets, split, *refs),
        in_specs=[smem()] + vmem(len(near)),
        out_specs=vmem(2),
        out_shape=[
            jax.ShapeDtypeStruct((len(reach), *piece.shape), jnp.bfloat16),
            jax.ShapeDtypeStruct((4 * rows, segments * LANES), jnp.bfloat16),
        ],
        compiler_params=pltpu.CompilerParams(vmem_limit_bytes=10 * MIB),
        cost_estimate=pl.CostEstimate(
            flops=2 * len(offsets) * 4 * rows * 2 * rows * segments * LANES,
            bytes_accessed=4 * MIB,
            transcendentals=0,
        ),
        name="near",
    )(here, *near)
    shares = pl.pallas_call(
        lambda *refs: far_kernel(scale, ring, reach, len(far), *refs),
        in_specs=[smem()] + vmem(2 + len(far)),
        out_specs=vmem(len(reach)),
        out_shape=[piece] * len(reach),
        compiler_params=pltpu.CompilerParams(vmem_limit_bytes=10 * MIB),
        name="far",
    )(here, products, left, *far)
    pieces = []
    for (dx, dy), share in zip(reach, shares, strict=True):
        if dx or dy:
            route = [
                (x * segments + y, (x + dx) % sides * segments + (y + dy) % segments)
                for x in range(sides)
                for y in range(segments)
            ]
            share = lax.ppermute(share, ("xhi", "y"), route)
        pieces.append(share)

    def store(numbers, before):
        return pl.pallas_call(
            lambda *refs: store_kernel([reach[k] for k in numbers], *refs),
            in_specs=[smem()]
            + vmem(len(numbers))
            + [pl.BlockSpec(memory_space=pl.ANY)] * len(before),
            out_specs=pl.BlockSpec(memory_space=pl.ANY),
            out_shape=jax.ShapeDtypeStruct((2, len(reach), rows, 4 * rows), jnp.float32),
            scratch_shapes=[
                pltpu.VMEM((len(numbers), 2, rows, 4 * rows), jnp.float32),
                pltpu.SemaphoreType.DMA((len(numbers), 2)),
            ],
            input_output_aliases={1 + len(numbers): 0} if before else {},
            compiler_params=pltpu.CompilerParams(vmem_limit_bytes=10 * MIB),
            name="store",
        )(here, *[pieces[k] for k in numbers], *before)

    part = store((7, 0, 1), ())
    part = store((2, 3, 4), (part,))
    return store((5, 6), (part,))


def solution(mesh):
    fine = Mesh(mesh.devices.reshape(2, 2, 8, 2, 4), ("xlo", "core", "z", "xhi", "y"))
    return jax.shard_map(
        body,
        mesh=fine,
        in_specs=(P(("z", "xhi"), ("xlo", "core"), "y"), P()),
        out_specs=P(None, ("xlo", "core"), ("z", "xhi"), "y"),
        check_vma=False,
    )
```
